512 devices in a mesh: frame: 64 (over z, x, core), head: 8 (over y).
Axes of the slice: x: 4, y: 8, z: 8, core: 2. Of those that a mesh axis runs over, the one named last changes fastest.
Arguments:
- queries: bfloat16 [32768, 3072], P(('frame', 'head')), may hold values from -80 to 80
- keys: bfloat16 [32768, 3072], P(('frame', 'head')), may hold values from -80 to 80
- values: bfloat16 [32768, 3072], P(('frame', 'head')), may hold values from -6 to 6
- q_gain: float32 [3072], replicated, may hold values from 0.5 to 2
- k_gain: float32 [3072], replicated, may hold values from 0.5 to 2
- block_offset: int32 [64, 3, 2], replicated, may hold values from 0 to 3, as said below
Outputs:
- attended: bfloat16 [32768, 3072], P(('frame', 'head'))
The draws below stay inside these ranges and needn't reach their ends.
Inputs may be any that keep to these rules, and one draw needn't show every extreme that they name: block_offset[f, l, s] is below 2 ** l.
All inputs are finite; a program needn't handle non-finite values.
Results may differ from the reference program's by a relative error of at most 0.012.
The reference program's roundings to bfloat16 on the way (of `q_norm`, `k_norm` and `weights`) count: a program that leaves them out, or rounds other values in their place, can miss the bound.
Values may be sent and summed in bfloat16 or wider, within the bound.
No kernel may reach another device: no remote copies, remote signals or barrier semaphores. Data moves between devices by JAX's collectives and lax.ppermute only.
A program may use at most 128 MiB of HBM per device.

```python
import math
import jax
import jax.numpy as jnp
from jax import lax

HEADS = 24
HD = 128
NBLK = 8
LEVELS = 3
TOK_DEV = 64
NFRAMES = 64
TOKENS = 32768
WIDTH = 3072
N_HEAD = 8


def draw_queries(key, part):
    key = jax.random.fold_in(key, 11)
    result = jax.random.normal(key, (TOKENS, HEADS * HD), jnp.float32)
    return jnp.clip(result, -80.0, 80.0).astype(jnp.bfloat16)


def draw_keys(key, part):
    key = jax.random.fold_in(key, 23)
    result = jax.random.normal(key, (TOKENS, HEADS * HD), jnp.float32)
    return jnp.clip(result, -80.0, 80.0).astype(jnp.bfloat16)


def draw_block_offset(key, part):
    key = jax.random.fold_in(key, 37)
    periods = 2 ** jnp.arange(LEVELS, dtype=jnp.int32)
    random_bits = jax.random.randint(key, (NFRAMES, LEVELS, 2), 0, 2 ** 30, dtype=jnp.int32)
    table = random_bits % periods[None, :, None]
    table = table.at[0, LEVELS - 1, 1].set(2 ** (LEVELS - 1) - 1)
    return table.astype(jnp.int32)


def levels(key, extent, shards, smallest, top_value):
    level, own = 1.0, jax.random.fold_in(key, 6)
    for position, shards_of in shards:
        steps = jnp.exp(jax.random.uniform(jax.random.fold_in(own, position), (shards_of,), jnp.float32, smallest / len(shards), top_value / len(shards)))
        level = level * jnp.repeat(steps, extent[position] // shards_of).reshape([-1 if axis == position else 1 for axis in range(len(extent))])
    return level


def normal_values(key, shape, deviation, limit, pieces=(), kind=jnp.bfloat16):
    gain = levels(key, shape, pieces, -0.22, 0.18) if pieces else 1.0
    values = jax.random.normal(key, shape, jnp.float32) * deviation * gain
    return jnp.minimum(jnp.maximum(values, -limit), limit).astype(kind)


def setup_inputs(seed: int = 0) -> dict:
    arg_keys = jax.random.split(jax.random.key(seed), 7)
    return {
        "queries": draw_queries(jax.random.fold_in(arg_keys[6], 71), 0),
        "keys": draw_keys(jax.random.fold_in(arg_keys[6], 71), 0),
        "values": normal_values(arg_keys[2], (TOKENS, WIDTH), 1.0, 6.0, ((0, 512),)),
        "q_gain": jnp.clip(jax.random.uniform(arg_keys[3], (WIDTH,), jnp.float32, 0.5, 2.0), 0.5, 2.0),
        "k_gain": jnp.clip(jax.random.uniform(arg_keys[4], (WIDTH,), jnp.float32, 0.5, 2.0), 0.5, 2.0),
        "block_offset": draw_block_offset(jax.random.fold_in(arg_keys[6], 71), 0),
    }


def normalize(matrix, gain_row):
    as_float = matrix.astype(jnp.float32)
    mean_square = lax.optimization_barrier(jnp.mean(as_float * as_float, axis=-1, keepdims=True))
    return (as_float * lax.rsqrt(mean_square + 1e-06) * gain_row).astype(jnp.bfloat16)

def reference(queries, keys, values, q_gain, k_gain, block_offset):
    frame_len = TOK_DEV * N_HEAD
    block_len = frame_len // NBLK
    q_norm = normalize(queries, q_gain).reshape(NFRAMES, frame_len, HEADS, HD)
    k_norm = normalize(keys, k_gain).reshape(NFRAMES, frame_len, HEADS, HD)
    v_all = values.reshape(NFRAMES, frame_len, HEADS, HD)
    score_scale = 1.0 / math.sqrt(HD)
    block_ids = (jnp.arange(frame_len, dtype=jnp.int32) // block_len).astype(jnp.int32)

    def one_frame(frame_now):
        key_parts = [lax.dynamic_index_in_dim(k_norm, frame_now, 0, keepdims=False)]
        value_parts = [lax.dynamic_index_in_dim(v_all, frame_now, 0, keepdims=False)]
        keep_parts = [jnp.ones((frame_len, frame_len), dtype=bool)]
        for level_now in range(LEVELS):
            stride = 2 ** level_now
            for facing in range(2):
                offset = block_offset[frame_now, level_now, facing].astype(jnp.int32)
                pattern = (block_ids[None, :] - block_ids[:, None] - offset) % stride == 0
                for distance in range(stride, 2 * stride):
                    source = frame_now - distance if facing == 0 else frame_now + distance
                    usable = (source >= 0) & (source < NFRAMES)
                    clipped = jnp.clip(source, 0, NFRAMES - 1).astype(jnp.int32)
                    key_parts.append(lax.dynamic_index_in_dim(k_norm, clipped, 0, keepdims=False))
                    value_parts.append(lax.dynamic_index_in_dim(v_all, clipped, 0, keepdims=False))
                    keep_parts.append(pattern & usable)
        key_all = jnp.concatenate(key_parts, axis=0).transpose(1, 0, 2)
        value_all = jnp.concatenate(value_parts, axis=0).transpose(1, 0, 2)
        keep_all = jnp.concatenate(keep_parts, axis=1)
        query_now = lax.dynamic_index_in_dim(q_norm, frame_now, 0, keepdims=False).transpose(1, 0, 2)

        def one_head(inputs):
            query_head, key_head, value_head = inputs
            scores = jnp.dot(query_head, key_head.T, preferred_element_type=jnp.float32) * score_scale
            scores = jnp.where(keep_all, scores, -1e+30)
            row_top = lax.optimization_barrier(jnp.max(scores, axis=1, keepdims=True))
            weights = jnp.where(keep_all, jnp.exp(scores - row_top), 0.0)
            row_total = lax.optimization_barrier(jnp.sum(weights, axis=1, keepdims=True))
            row_mixed = jnp.dot(weights.astype(jnp.bfloat16), value_head, preferred_element_type=jnp.float32)
            return (row_mixed / row_total).astype(jnp.bfloat16)
        return lax.map(one_head, (query_now, key_all, value_all))
    frames_out = lax.map(one_frame, jnp.arange(NFRAMES, dtype=jnp.int32))
    return frames_out.transpose(0, 2, 1, 3).reshape(TOKENS, HEADS * HD)
```

```python
import math

import jax
import jax.numpy as jnp
from jax import lax
from jax.experimental import pallas as pl
from jax.experimental.pallas import tpu as pltpu
from jax.sharding import Mesh
from jax.sharding import PartitionSpec as P

HD = 128
HEADS = 24
TOK = 64
SLOTS = 32
LOG2E = 1.4426950408889634
FACTOR = LOG2E / math.sqrt(HD)
VMEM_LIMIT = 48 * 1024 * 1024
WHOLE = pl.BlockSpec(memory_space=pltpu.VMEM)
TABLE = pl.BlockSpec(memory_space=pltpu.SMEM)
ANYWHERE = pl.BlockSpec(memory_space=pl.ANY)


THEIRS = 13
ZERO = 25
OWN_FLOPS = 40 * 8704 * 512 * HD
FRAMES = 26
DISTANCES = (0, 1, -1, 2, -2, 3, -3, 4, -4, 6, -6, 5, -5, 7, -7)


def normed(x_ref, gain_ref):
    x = x_ref[...].astype(jnp.float32)
    mean_square = jnp.mean(x * x, axis=-1, keepdims=True)
    return (x * lax.rsqrt(mean_square + 1e-06) * gain_ref[...]).astype(jnp.bfloat16)


def spread(x, out_ref):
    for h in range(HEADS):
        out_ref[h] = x[:, h * HD : (h + 1) * HD]
    for h in range(HEADS, SLOTS):
        out_ref[h] = jnp.zeros(out_ref.shape[1:], out_ref.dtype)


def prepare_kv(k_ref, v_ref, gain_ref, out_ref):
    spread(normed(k_ref, gain_ref), out_ref.at[:, 0])
    spread(v_ref, out_ref.at[:, 1])


def prepare_q(q_ref, gain_ref, out_ref):
    spread(normed(q_ref, gain_ref), out_ref)


def lane_fold(op, matrix):
    parts = [matrix[:, n : n + HD] for n in range(0, matrix.shape[1], HD)]
    while len(parts) > 1:
        parts = [op(*parts[n : n + 2]) if n + 1 < len(parts) else parts[n] for n in range(0, len(parts), 2)]
    return parts[0]


def width(d):
    return 512 if abs(d) <= 1 else 256 if abs(d) <= 3 else 128


def place(i, d):
    if d % 2 == 0:
        n = 4 + i + d // 2
        return n, "low" if n < 4 else "high" if n >= 8 else None
    n = 4 + i + (d - 1) // 2
    return THEIRS + n, "low" if n < 3 else "edge_low" if n == 3 else "high" if n >= 8 else "edge_high" if n == 7 else None


class Unit:
    def __init__(self, meta_ref, i, parity, inside, keys, values):
        self.i = i
        self.parity = parity
        self.offs = [[meta_ref[2 + (i * 3 + level) * 2 + side] for side in range(2)] for level in range(3)]
        self.keys = keys
        self.values = values
        used = [d for d in DISTANCES if (place(i, d)[1] is None) == inside]
        self.both = []
        self.far = []
        for size, groups in ((512, self.both), (256, self.both), (128, self.far)):
            here = [d for d in used if width(d) == size]
            per = 512 // size
            groups += [here[n : n + per] for n in range(0, len(here), per)]

    def q(self, q_ref, high):
        return q_ref[self.i, :, high, self.parity].reshape(HD, HD)

    def gather(self, fetch, group, cls):
        parts = []
        for d in group:
            side = 0 if d < 0 else 1
            if abs(d) <= 1:
                at = (slice(None),) * 3
            elif abs(d) <= 3:
                at = (slice(None), slice(None), (cls + self.offs[1][side]) & 1)
            else:
                kept = (cls + self.offs[2][side]) & 3
                at = (slice(None), kept >> 1, kept & 1)
            parts.append(fetch(self.i, d, at).reshape(width(d), HD))
        return jnp.concatenate(parts, axis=0)


def score(unit, q_ref, s_ref, before=None):
    q = [unit.q(q_ref, high) for high in range(2)]
    both = jnp.concatenate(q, axis=0)
    contract = (((1,), (1,)), ((), ()))
    top = before
    start = 0
    for group in unit.both:
        key = unit.gather(unit.keys, group, unit.parity)
        s = lax.dot_general(both, key, contract, preferred_element_type=jnp.float32)
        s_ref[:, start : start + key.shape[0]] = s
        start += key.shape[0]
        part = lane_fold(jnp.maximum, s)
        top = part if top is None else jnp.maximum(top, part)
    tops = []
    for high in range(2):
        rows = slice(high * HD, (high + 1) * HD)
        own = top[rows]
        at = start
        for group in unit.far:
            key = unit.gather(unit.keys, group, unit.parity + 2 * high)
            s = lax.dot_general(q[high], key, contract, preferred_element_type=jnp.float32)
            s_ref[rows, at : at + key.shape[0]] = s
            at += key.shape[0]
            own = jnp.maximum(own, lane_fold(jnp.maximum, s))
        tops.append(jnp.max(own, axis=1, keepdims=True))
    return tops


def mix(unit, tops, s_ref, flags):
    shift = jnp.concatenate(tops, axis=0) * FACTOR
    sums = {}

    def weigh(rows, start, group, moved):
        size = width(group[0])
        weights = jnp.exp2(s_ref[rows, start : start + size * len(group)] * FACTOR - moved)
        for m, d in enumerate(group):
            part = lane_fold(jnp.add, weights[:, m * size : (m + 1) * size])
            key = (place(unit.i, d)[1], rows.start, rows.stop)
            sums[key] = sums[key] + part if key in sums else part
        return weights.astype(jnp.bfloat16)

    total = None
    start = 0
    for group in unit.both:
        w = weigh(slice(0, 256), start, group, shift)
        start += w.shape[1]
        mixed = jnp.dot(w, unit.gather(unit.values, group, unit.parity), preferred_element_type=jnp.float32)
        total = mixed if total is None else total + mixed
    result = []
    for high in range(2):
        rows = slice(high * HD, (high + 1) * HD)
        own = total[rows]
        at = start
        for group in unit.far:
            w = weigh(rows, at, group, shift[rows])
            at += w.shape[1]
            value = unit.gather(unit.values, group, unit.parity + 2 * high)
            own = own + jnp.dot(w, value, preferred_element_type=jnp.float32)
        lanes = None
        for (kind, first, last), part in sums.items():
            if not first <= rows.start < last:
                continue
            if last - first == 256:
                part = part[rows]
            if kind is not None:
                part = part * flags[kind]
            lanes = part if lanes is None else lanes + part
        result.append((lanes, own))
    return result


def attend_own(meta_ref, q_ref, mine_ref, theirs_ref, top_ref, lanes_ref, total_ref, s_even, s_odd):
    core = meta_ref[1]

    def fetch(which):
        def of(i, d, at):
            n = place(i, d)[0]
            ref, n = (mine_ref, n - 4) if d % 2 == 0 else (theirs_ref, n - THEIRS - 4 + core)
            return ref[(n,) + at + (which,)]

        return of

    units = [Unit(meta_ref, i, parity, True, fetch(0), fetch(1)) for i in range(4) for parity in range(2)]
    s_refs = (s_even, s_odd)
    tops = score(units[0], q_ref, s_refs[0])
    for n, unit in enumerate(units):
        now = tops
        if n + 1 < len(units):
            tops = score(units[n + 1], q_ref, s_refs[(n + 1) % 2])
        for high, (lanes, own) in enumerate(mix(unit, now, s_refs[n % 2], None)):
            rows = slice(high * HD, (high + 1) * HD)
            top_ref[n, rows] = jnp.broadcast_to(now[high], (HD, HD))
            lanes_ref[n, rows] = lanes
            total_ref[n, rows] = own


def attend_rest(
    meta_ref, q_ref, top_ref, lanes_ref, total_ref, own, low, high_ref, their_own, their_low, their_high,
    out_ref, k_ref, v_ref, s_even, s_odd, sems,
):
    z = meta_ref[0]
    core = meta_ref[1]
    sources = ((low, 0), (high_ref, 8), (their_low, THEIRS - core), (their_own, THEIRS - core + 4),
               (their_high, THEIRS - core + 8))

    def copy(src, which, ref, slot, n):
        made = pltpu.make_async_copy(src.at[:, :, :, :, which], ref.at[pl.ds(slot, 4)], sems.at[n])
        made.start()
        return made

    k_copies = [copy(src, 0, k_ref, slot, n) for n, (src, slot) in enumerate(sources + ((own, 4),))]
    v_copies = [copy(src, 1, v_ref, slot, n + 6) for n, (src, slot) in enumerate(sources)]
    v_ref[ZERO] = jnp.zeros(v_ref.shape[1:], v_ref.dtype)
    flag = lambda cond: jnp.where(cond, 1.0, 0.0).astype(jnp.float32)
    flags = {
        "low": flag(z > 0),
        "edge_low": flag((z > 0) | (core == 1)),
        "edge_high": flag((z < 7) | (core == 0)),
        "high": flag(z < 7),
    }

    def slot(i, d, outside):
        n, kind = place(i, d)
        return jnp.where(flags[kind] > 0, n, outside)

    def keys(i, d, at):
        return k_ref[(slot(i, d, 4 + i),) + at]

    def values(i, d, at):
        return v_ref[(slot(i, d, ZERO),) + at]

    units = [Unit(meta_ref, i, parity, False, keys, values) for i in range(4) for parity in range(2)]
    s_refs = (s_even, s_odd)
    for made in k_copies:
        made.wait()
    tops = score(units[0], q_ref, s_refs[0], top_ref[0])
    for made in v_copies:
        made.wait()
    for n, unit in enumerate(units):
        now = tops
        if n + 1 < len(units):
            tops = score(units[n + 1], q_ref, s_refs[(n + 1) % 2], top_ref[n + 1])
        for high, (lanes, mixed) in enumerate(mix(unit, now, s_refs[n % 2], flags)):
            rows = slice(high * HD, (high + 1) * HD)
            carried = jnp.exp2((top_ref[n, rows] - now[high]) * FACTOR)
            lanes = lanes + lanes_ref[n, rows] * carried
            mixed = mixed + total_ref[n, rows] * carried
            row_sum = jnp.sum(lanes, axis=1, keepdims=True)
            out_ref[unit.i, :, high, unit.parity] = (mixed / row_sum).astype(jnp.bfloat16).reshape(2, TOK, HD)


def side_by_side(x_ref, out_ref):
    for h in range(HEADS):
        out_ref[:, h * HD : (h + 1) * HD] = x_ref[h]


def call(kernel, out_shape, specs, flops=0, scratch=(), **more):
    params = pltpu.CompilerParams(vmem_limit_bytes=VMEM_LIMIT)
    cost = pl.CostEstimate(flops=flops, bytes_accessed=4 << 20, transcendentals=flops // 512)
    return pl.pallas_call(
        kernel, out_shape=out_shape, in_specs=specs, scratch_shapes=scratch,
        compiler_params=params, cost_estimate=cost, **more,
    )


def exchange(x):
    return lax.all_to_all(x, ("x", "y"), split_axis=0, concat_axis=0, tiled=True)


def local(queries, keys, values, q_gain, k_gain, block_offset):
    half = jnp.bfloat16
    z = lax.axis_index("z")
    core = lax.axis_index("c")
    frame = lax.dynamic_slice_in_dim(block_offset.reshape(8, 4, 2, 6), z, 1, 0)
    table = lax.dynamic_slice_in_dim(frame, core, 1, 2).reshape(24)
    meta = jnp.concatenate([jnp.stack([z, core]).astype(jnp.int32), table])

    kv = call(prepare_kv, jax.ShapeDtypeStruct((SLOTS, 2, TOK, HD), half), [WHOLE] * 3)(
        keys, values, k_gain.reshape(1, -1)
    )
    queries, kv = lax.optimization_barrier((queries, kv))
    q = call(prepare_q, jax.ShapeDtypeStruct((SLOTS, TOK, HD), half), [WHOLE] * 2)(queries, q_gain.reshape(1, -1))
    kv = exchange(kv)
    q, kv = lax.optimization_barrier((q, kv))
    blocks = (4, 2, 2, 2, TOK, HD)
    q = exchange(q).reshape(blocks)

    mine = kv.reshape(4, 2, 2, 2, 2, TOK, HD)
    swap = [(0, 1), (1, 0)]
    low = lax.ppermute(mine, "z", [(n, n + 1) for n in range(7)])
    high = lax.ppermute(mine, "z", [(n + 1, n) for n in range(7)])
    theirs = lax.ppermute(mine, "c", swap)
    their_low = lax.ppermute(low, "c", swap)
    their_high = lax.ppermute(high, "c", swap)

    scores = [pltpu.VMEM((256, 2560), jnp.float32)] * 2
    state = [jax.ShapeDtypeStruct((8, 256, HD), jnp.float32)] * 3
    state = call(attend_own, state, [TABLE] + [WHOLE] * 3, flops=OWN_FLOPS, scratch=scores)(meta, q, mine, theirs)
    kept = pltpu.VMEM((FRAMES, 2, 2, 2, TOK, HD), half)
    out = call(
        attend_rest,
        jax.ShapeDtypeStruct(blocks, half),
        [TABLE] + [WHOLE] * 4 + [ANYWHERE] * 6,
        flops=4 * 5632 * 512 * HD,
        scratch=[kept, kept] + scores + [pltpu.SemaphoreType.DMA((11,))],
    )(meta, q, *state, mine, low, high, theirs, their_low, their_high)
    back = exchange(out.reshape(SLOTS, TOK, HD))
    return call(side_by_side, jax.ShapeDtypeStruct((TOK, HEADS * HD), half), [WHOLE])(back)


def solution(mesh):
    grid = Mesh(mesh.devices.reshape(8, 4, 2, 8), ("z", "x", "c", "y"))
    tokens = P(("z", "x", "c", "y"), None)
    return jax.shard_map(
        local, mesh=grid, in_specs=(tokens,) * 3 + (P(),) * 3, out_specs=tokens, check_vma=False
    )
```

```python
import math

import jax
import jax.numpy as jnp
from jax import lax
from jax.experimental import pallas as pl
from jax.experimental.pallas import tpu as pltpu
from jax.sharding import Mesh
from jax.sharding import PartitionSpec as P

HD = 128
HEADS = 24
TOK = 64
SLOTS = 32
LOG2E = 1.4426950408889634
FACTOR = LOG2E / math.sqrt(HD)
VMEM_LIMIT = 48 * 1024 * 1024
PREPARE_LIMIT = 60 * 1024 * 1024
WHOLE = pl.BlockSpec(memory_space=pltpu.VMEM)
TABLE = pl.BlockSpec(memory_space=pltpu.SMEM)
ANYWHERE = pl.BlockSpec(memory_space=pl.ANY)


DISTANCES = (0, 1, -1, 2, -2, 3, -3, 4, -4, 6, -6, 5, -5, 7, -7)


def normed(x_ref, gain_ref):
    x = x_ref[...].astype(jnp.float32)
    mean_square = jnp.mean(x * x, axis=-1, keepdims=True)
    return (x * lax.rsqrt(mean_square + 1e-06) * gain_ref[...]).astype(jnp.bfloat16)


def spread(x, out_ref):
    for h in range(HEADS):
        out_ref[h] = x[:, h * HD : (h + 1) * HD]
    for h in range(HEADS, SLOTS):
        out_ref[h] = jnp.zeros(out_ref.shape[1:], out_ref.dtype)


def prepare_kv(k_hbm, v_hbm, gain_hbm, out_ref, k_ref, v_ref, gain_ref, sems):
    pairs = ((k_hbm, k_ref), (gain_hbm, gain_ref), (v_hbm, v_ref))
    loads = [pltpu.make_async_copy(src, dst, sems.at[n]) for n, (src, dst) in enumerate(pairs)]
    for load in loads:
        load.start()
    loads[0].wait()
    loads[1].wait()
    spread(normed(k_ref, gain_ref), out_ref.at[:, 0])
    loads[2].wait()
    spread(v_ref, out_ref.at[:, 1])


def prepare_q(q_ref, gain_ref, out_ref):
    spread(normed(q_ref, gain_ref), out_ref)


def lane_fold(op, matrix):
    parts = [matrix[:, n : n + HD] for n in range(0, matrix.shape[1], HD)]
    while len(parts) > 1:
        parts = [op(*parts[n : n + 2]) if n + 1 < len(parts) else parts[n] for n in range(0, len(parts), 2)]
    return parts[0]


def width(d):
    return 512 if abs(d) <= 1 else 256 if abs(d) <= 3 else 128


def place(i, d):
    if d % 2 == 0:
        n = 4 + i + d // 2
        return n, "low" if n < 4 else "high" if n >= 8 else None
    n = 4 + i + (d - 1) // 2
    return n, "low" if n < 3 else "edge_low" if n == 3 else "high" if n >= 8 else "edge_high" if n == 7 else None


class Unit:
    def __init__(self, meta_ref, i, parity, odd, keys, values):
        self.i = i
        self.parity = parity
        self.offs = [[meta_ref[2 + (i * 3 + level) * 2 + side] for side in range(2)] for level in range(3)]
        self.keys = keys
        self.values = values
        used = [d for d in DISTANCES if d % 2 == odd]
        self.both = []
        self.far = []
        for size, groups in ((512, self.both), (256, self.both), (128, self.far)):
            here = [d for d in used if width(d) == size]
            per = 512 // size
            groups += [here[n : n + per] for n in range(0, len(here), per)]

    def q(self, q_ref, high):
        return q_ref[self.i, :, high, self.parity].reshape(HD, HD)

    def gather(self, fetch, group, cls):
        parts = []
        for d in group:
            side = 0 if d < 0 else 1
            if abs(d) <= 1:
                at = (slice(None),) * 3
            elif abs(d) <= 3:
                at = (slice(None), slice(None), (cls + self.offs[1][side]) & 1)
            else:
                kept = (cls + self.offs[2][side]) & 3
                at = (slice(None), kept >> 1, kept & 1)
            parts.append(fetch(self.i, d, at).reshape(width(d), HD))
        return jnp.concatenate(parts, axis=0)


def store_scores(unit, q, group, cls, s_ref, rows, start, bias):
    key = unit.gather(unit.keys, group, cls)
    s = lax.dot_general(q, key, (((1,), (1,)), ((), ())), preferred_element_type=jnp.float32)
    size = width(group[0])
    parts = [s[:, m * size : (m + 1) * size] for m in range(len(group))]
    for m, d in enumerate(group):
        kind = place(unit.i, d)[1]
        parts[m] = parts[m] if kind is None else parts[m] + bias[kind]
    s = jnp.concatenate(parts, axis=1)
    s_ref[rows, start : start + key.shape[0]] = s
    return lane_fold(jnp.maximum, s), start + key.shape[0]


def score(unit, q_ref, s_ref, bias, before=None):
    q = [unit.q(q_ref, high) for high in range(2)]
    both = jnp.concatenate(q, axis=0)
    top = before
    start = 0
    for group in unit.both:
        part, start = store_scores(unit, both, group, unit.parity, s_ref, slice(0, 256), start, bias)
        top = part if top is None else jnp.maximum(top, part)
    tops = []
    for high in range(2):
        rows = slice(high * HD, (high + 1) * HD)
        own = top[rows]
        at = start
        for group in unit.far:
            part, at = store_scores(unit, q[high], group, unit.parity + 2 * high, s_ref, rows, at, bias)
            own = jnp.maximum(own, part)
        tops.append(jnp.max(own, axis=1, keepdims=True))
    return tops


def mix(unit, tops, s_ref):
    shift = jnp.concatenate(tops, axis=0) * FACTOR
    sums = {}

    def weigh(rows, start, group, moved):
        size = width(group[0])
        weights = jnp.exp2(s_ref[rows, start : start + size * len(group)] * FACTOR - moved)
        key = (rows.start, rows.stop)
        for m in range(len(group)):
            part = lane_fold(jnp.add, weights[:, m * size : (m + 1) * size])
            sums[key] = sums[key] + part if key in sums else part
        return weights.astype(jnp.bfloat16)

    total = None
    start = 0
    for group in unit.both:
        w = weigh(slice(0, 256), start, group, shift)
        start += w.shape[1]
        mixed = jnp.dot(w, unit.gather(unit.values, group, unit.parity), preferred_element_type=jnp.float32)
        total = mixed if total is None else total + mixed
    result = []
    for high in range(2):
        rows = slice(high * HD, (high + 1) * HD)
        own = total[rows]
        at = start
        for group in unit.far:
            w = weigh(rows, at, group, shift[rows])
            at += w.shape[1]
            value = unit.gather(unit.values, group, unit.parity + 2 * high)
            own = own + jnp.dot(w, value, preferred_element_type=jnp.float32)
        lanes = None
        for (first, last), part in sums.items():
            if not first <= rows.start < last:
                continue
            if last - first == 256:
                part = part[rows]
            lanes = part if lanes is None else lanes + part
        result.append((lanes, own))
    return result


def biases(meta_ref):
    z = meta_ref[0]
    core = meta_ref[1]
    usable = {
        "low": z > 0,
        "edge_low": (z > 0) | (core == 1),
        "edge_high": (z < 7) | (core == 0),
        "high": z < 7,
    }
    return {kind: jnp.where(inside, 0.0, -1e30).astype(jnp.float32) for kind, inside in usable.items()}


def attend_mine(meta_ref, q_ref, low, own_ref, high_ref, top_ref, lanes_ref, total_ref, s_even, s_odd):
    bias = biases(meta_ref)

    def fetch(which):
        def of(i, d, at):
            n = place(i, d)[0]
            return (low, own_ref, high_ref)[n // 4][(n % 4,) + at + (which,)]

        return of

    units = [Unit(meta_ref, i, parity, 0, fetch(0), fetch(1)) for i in range(4) for parity in range(2)]
    s_refs = (s_even, s_odd)
    tops = score(units[0], q_ref, s_refs[0], bias)
    for n, unit in enumerate(units):
        now = tops
        if n + 1 < len(units):
            tops = score(units[n + 1], q_ref, s_refs[(n + 1) % 2], bias)
        for high, (lanes, own) in enumerate(mix(unit, now, s_refs[n % 2])):
            rows = slice(high * HD, (high + 1) * HD)
            top_ref[n, rows] = jnp.broadcast_to(now[high], (HD, HD))
            lanes_ref[n, rows] = lanes
            total_ref[n, rows] = own


def attend_theirs(
    meta_ref, q_ref, top_ref, lanes_ref, total_ref, low, own_ref, high_ref, out_ref, k_ref, v_ref, s_even, s_odd, sems
):
    first = 1 - meta_ref[1]
    sources = ((low, first), (own_ref, first + 4), (high_ref, first + 8))

    def load(src, which, ref, slot, n):
        made = pltpu.make_async_copy(src.at[:, :, :, :, which], ref.at[pl.ds(slot, 4)], sems.at[n])
        made.start()
        return made

    k_copies = [load(src, 0, k_ref, slot, n) for n, (src, slot) in enumerate(sources)]
    v_copies = [load(src, 1, v_ref, slot, n + 3) for n, (src, slot) in enumerate(sources)]
    bias = biases(meta_ref)

    def keys(i, d, at):
        return k_ref[(place(i, d)[0] + 1,) + at]

    def values(i, d, at):
        return v_ref[(place(i, d)[0] + 1,) + at]

    units = [Unit(meta_ref, i, parity, 1, keys, values) for i in range(4) for parity in range(2)]
    s_refs = (s_even, s_odd)
    for made in k_copies:
        made.wait()
    tops = score(units[0], q_ref, s_refs[0], bias, top_ref[0])
    for made in v_copies:
        made.wait()
    for n, unit in enumerate(units):
        now = tops
        if n + 1 < len(units):
            tops = score(units[n + 1], q_ref, s_refs[(n + 1) % 2], bias, top_ref[n + 1])
        for high, (lanes, mixed) in enumerate(mix(unit, now, s_refs[n % 2])):
            rows = slice(high * HD, (high + 1) * HD)
            carried = jnp.exp2((top_ref[n, rows] - now[high]) * FACTOR)
            lanes = lanes + lanes_ref[n, rows] * carried
            mixed = mixed + total_ref[n, rows] * carried
            row_sum = jnp.sum(lanes, axis=1, keepdims=True)
            out_ref[unit.i, :, high, unit.parity] = (mixed / row_sum).astype(jnp.bfloat16).reshape(2, TOK, HD)


def side_by_side(x_ref, out_ref):
    for h in range(HEADS):
        out_ref[:, h * HD : (h + 1) * HD] = x_ref[h]


def call(kernel, out_shape, specs, flops=0, scratch=(), limit=VMEM_LIMIT, **more):
    params = pltpu.CompilerParams(vmem_limit_bytes=limit)
    cost = pl.CostEstimate(flops=flops, bytes_accessed=4 << 20, transcendentals=flops // 512)
    return pl.pallas_call(
        kernel, out_shape=out_shape, in_specs=specs, scratch_shapes=scratch,
        compiler_params=params, cost_estimate=cost, **more,
    )


def exchange(x):
    return lax.all_to_all(x, ("x", "y"), split_axis=0, concat_axis=0, tiled=True)


def local(queries, keys, values, q_gain, k_gain, block_offset):
    half = jnp.bfloat16
    z = lax.axis_index("z")
    core = lax.axis_index("c")
    frame = lax.dynamic_slice_in_dim(block_offset.reshape(8, 4, 2, 6), z, 1, 0)
    table = lax.dynamic_slice_in_dim(frame, core, 1, 2).reshape(24)
    meta = jnp.concatenate([jnp.stack([z, core]).astype(jnp.int32), table])

    tokens = pltpu.VMEM((TOK, HEADS * HD), half)
    kv = call(
        prepare_kv,
        jax.ShapeDtypeStruct((SLOTS, 2, TOK, HD), half),
        [ANYWHERE] * 3,
        scratch=[tokens, tokens, pltpu.VMEM((1, HEADS * HD), jnp.float32), pltpu.SemaphoreType.DMA((3,))],
        limit=PREPARE_LIMIT,
    )(keys, values, k_gain.reshape(1, -1))
    queries, kv = lax.optimization_barrier((queries, kv))
    q = call(prepare_q, jax.ShapeDtypeStruct((SLOTS, TOK, HD), half), [WHOLE] * 2)(queries, q_gain.reshape(1, -1))
    kv = exchange(kv)
    q, kv = lax.optimization_barrier((q, kv))
    blocks = (4, 2, 2, 2, TOK, HD)
    q = exchange(q).reshape(blocks)

    mine = kv.reshape(4, 2, 2, 2, 2, TOK, HD)
    swap = [(0, 1), (1, 0)]
    low = lax.ppermute(mine, "z", [(n, n + 1) for n in range(7)])
    high = lax.ppermute(mine, "z", [(n + 1, n) for n in range(7)])
    theirs = lax.ppermute(mine, "c", swap)
    their_low = lax.ppermute(low, "c", swap)
    their_high = lax.ppermute(high, "c", swap)

    state = [jax.ShapeDtypeStruct((8, 256, HD), jnp.float32)] * 3
    state = call(
        attend_mine,
        state,
        [TABLE] + [WHOLE] * 4,
        flops=4 * 4 * 1536 * 512 * HD,
        scratch=[pltpu.VMEM((256, 1536), jnp.float32)] * 2,
    )(meta, q, low, mine, high)
    kept = pltpu.VMEM((13, 2, 2, 2, TOK, HD), half)
    out = call(
        attend_theirs,
        jax.ShapeDtypeStruct(blocks, half),
        [TABLE] + [WHOLE] * 4 + [ANYWHERE] * 3,
        flops=4 * 4 * 2048 * 512 * HD,
        scratch=[kept, kept] + [pltpu.VMEM((256, 2048), jnp.float32)] * 2 + [pltpu.SemaphoreType.DMA((6,))],
    )(meta, q, *state, their_low, theirs, their_high)
    back = exchange(out.reshape(SLOTS, TOK, HD))
    return call(side_by_side, jax.ShapeDtypeStruct((TOK, HEADS * HD), half), [WHOLE])(back)


def solution(mesh):
    grid = Mesh(mesh.devices.reshape(8, 4, 2, 8), ("z", "x", "c", "y"))
    tokens = P(("z", "x", "c", "y"), None)
    return jax.shard_map(
        local, mesh=grid, in_specs=(tokens,) * 3 + (P(),) * 3, out_specs=tokens, check_vma=False
    )
```

```python
import itertools
import math

import jax
import jax.numpy as jnp
from jax import lax
from jax.experimental import pallas as pl
from jax.experimental.pallas import tpu as pltpu
from jax.sharding import Mesh
from jax.sharding import PartitionSpec as P

HD = 128
HEADS = 24
TOK = 64
SLOTS = 32
LOG2E = 1.4426950408889634
FACTOR = LOG2E / math.sqrt(HD)
VMEM_LIMIT = 48 * 1024 * 1024
PREPARE_LIMIT = 60 * 1024 * 1024
WHOLE = pl.BlockSpec(memory_space=pltpu.VMEM)
TABLE = pl.BlockSpec(memory_space=pltpu.SMEM)
ANYWHERE = pl.BlockSpec(memory_space=pl.ANY)


META = 26
DISTANCES = (0, 1, -1, 2, -2, 3, -3, 4, -4, 6, -6, 5, -5, 7, -7)


def normed(x_ref, gain_ref):
    x = x_ref[...].astype(jnp.float32)
    mean_square = jnp.mean(x * x, axis=-1, keepdims=True)
    return (x * lax.rsqrt(mean_square + 1e-06) * gain_ref[...]).astype(jnp.bfloat16)


def spread(x, out_ref):
    for h in range(HEADS):
        out_ref[h] = x[:, h * HD : (h + 1) * HD]
    for h in range(HEADS, SLOTS):
        out_ref[h] = jnp.zeros(out_ref.shape[1:], out_ref.dtype)


def prepare_kv(k_hbm, v_hbm, gain_hbm, out_ref, k_ref, v_ref, gain_ref, sems):
    pairs = ((k_hbm, k_ref), (gain_hbm, gain_ref), (v_hbm, v_ref))
    loads = [pltpu.make_async_copy(src, dst, sems.at[n]) for n, (src, dst) in enumerate(pairs)]
    for load in loads:
        load.start()
    loads[0].wait()
    loads[1].wait()
    spread(normed(k_ref, gain_ref), out_ref.at[:, 0])
    loads[2].wait()
    spread(v_ref, out_ref.at[:, 1])


def prepare_q(q_ref, gain_ref, meta_ref, out_ref, meta_out):
    spread(normed(q_ref, gain_ref), out_ref)
    for n in range(META):
        meta_out[n] = meta_ref[n]


def lane_fold(op, matrix):
    parts = [matrix[:, n : n + HD] for n in range(0, matrix.shape[1], HD)]
    while len(parts) > 1:
        parts = [op(*parts[n : n + 2]) if n + 1 < len(parts) else parts[n] for n in range(0, len(parts), 2)]
    return parts[0]


def width(d):
    return 512 if abs(d) <= 1 else 256 if abs(d) <= 3 else 128


def place(i, d):
    if d % 2 == 0:
        n = 4 + i + d // 2
        return n, "low" if n < 4 else "high" if n >= 8 else None
    n = 4 + i + (d - 1) // 2
    return n, "low" if n < 3 else "edge_low" if n == 3 else "high" if n >= 8 else "edge_high" if n == 7 else None


class Unit:
    def __init__(self, meta_ref, i, parity, odd, keys, values):
        self.i = i
        self.parity = parity
        self.offs = [[meta_ref[2 + (i * 3 + level) * 2 + side] for side in range(2)] for level in range(3)]
        self.keys = keys
        self.values = values
        used = [d for d in DISTANCES if d % 2 == odd]
        self.both = []
        self.far = []
        for size, groups in ((512, self.both), (256, self.both), (128, self.far)):
            here = [d for d in used if width(d) == size]
            per = 512 // size
            groups += [here[n : n + per] for n in range(0, len(here), per)]

    def q(self, q_ref, high):
        return q_ref[self.i, :, high, self.parity].reshape(HD, HD)

    def gather(self, fetch, group, cls):
        parts = []
        for d in group:
            side = 0 if d < 0 else 1
            if abs(d) <= 1:
                at = (slice(None),) * 3
            elif abs(d) <= 3:
                at = (slice(None), slice(None), (cls + self.offs[1][side]) & 1)
            else:
                kept = (cls + self.offs[2][side]) & 3
                at = (slice(None), kept >> 1, kept & 1)
            parts.append(fetch(self.i, d, at).reshape(width(d), HD))
        return jnp.concatenate(parts, axis=0)


def store_scores(unit, q, group, cls, s_ref, rows, start, bias):
    key = unit.gather(unit.keys, group, cls)
    s = lax.dot_general(q, key, (((1,), (1,)), ((), ())), preferred_element_type=jnp.float32)
    size = width(group[0])
    parts = [s[:, m * size : (m + 1) * size] for m in range(len(group))]
    for m, d in enumerate(group):
        kind = place(unit.i, d)[1]
        parts[m] = parts[m] if kind is None else parts[m] + bias[kind]
    s = jnp.concatenate(parts, axis=1)
    s_ref[rows, start : start + key.shape[0]] = s
    return lane_fold(jnp.maximum, s), start + key.shape[0]


def score(unit, q_ref, s_ref, bias, before, tops):
    q = [unit.q(q_ref, high) for high in range(2)]
    both = jnp.concatenate(q, axis=0)
    top = before
    start = 0
    for group in unit.both:
        part, start = store_scores(unit, both, group, unit.parity, s_ref, slice(0, 256), start, bias)
        top = part if top is None else jnp.maximum(top, part)
        yield
    for high in range(2):
        rows = slice(high * HD, (high + 1) * HD)
        own = top[rows]
        at = start
        for group in unit.far:
            part, at = store_scores(unit, q[high], group, unit.parity + 2 * high, s_ref, rows, at, bias)
            own = jnp.maximum(own, part)
            yield
        tops.append(jnp.max(own, axis=1, keepdims=True))


def mix(unit, tops, s_ref, result):
    shift = jnp.concatenate(tops, axis=0) * FACTOR

    def weigh(rows, start, group, moved):
        size = width(group[0])
        weights = jnp.exp2(s_ref[rows, start : start + size * len(group)] * FACTOR - moved)
        return weights.astype(jnp.bfloat16), lane_fold(jnp.add, weights)

    total = None
    sums = None
    start = 0
    for group in unit.both:
        w, part = weigh(slice(0, 256), start, group, shift)
        start += w.shape[1]
        mixed = jnp.dot(w, unit.gather(unit.values, group, unit.parity), preferred_element_type=jnp.float32)
        total = mixed if total is None else total + mixed
        sums = part if sums is None else sums + part
        yield
    for high in range(2):
        rows = slice(high * HD, (high + 1) * HD)
        own = total[rows]
        lanes = sums[rows]
        at = start
        for group in unit.far:
            w, part = weigh(rows, at, group, shift[rows])
            at += w.shape[1]
            value = unit.gather(unit.values, group, unit.parity + 2 * high)
            own = own + jnp.dot(w, value, preferred_element_type=jnp.float32)
            lanes = lanes + part
            yield
        result.append((lanes, own))


def biases(meta_ref):
    z = meta_ref[0]
    core = meta_ref[1]
    usable = {
        "low": z > 0,
        "edge_low": (z > 0) | (core == 1),
        "edge_high": (z < 7) | (core == 0),
        "high": z < 7,
    }
    return {kind: jnp.where(inside, 0.0, -1e30).astype(jnp.float32) for kind, inside in usable.items()}


def units_of(meta_ref, odd, keys, values):
    return [Unit(meta_ref, i, parity, odd, keys, values) for i in range(4) for parity in range(2)]


def attend(units, q_ref, s_refs, bias, state, emit, late=None):
    before = lambda n: None if state is None else state[0][n]
    tops = []
    for _ in score(units[0], q_ref, s_refs[0], bias, before(0), tops):
        pass
    if late is not None:
        late()
    for n, unit in enumerate(units):
        now, tops, result = tops, [], []
        steps = [mix(unit, now, s_refs[n % 2], result)]
        if n + 1 < len(units):
            steps.insert(0, score(units[n + 1], q_ref, s_refs[(n + 1) % 2], bias, before(n + 1), tops))
        for _ in itertools.zip_longest(*steps):
            pass
        for high, (lanes, mixed) in enumerate(result):
            rows = slice(high * HD, (high + 1) * HD)
            if state is not None:
                carried = jnp.exp2((state[0][n, rows] - now[high]) * FACTOR)
                lanes = lanes + state[1][n, rows] * carried
                mixed = mixed + state[2][n, rows] * carried
            emit(n, rows, high, now[high], lanes, mixed)


def keep_in(top_ref, lanes_ref, total_ref):
    def emit(n, rows, high, top, lanes, mixed):
        top_ref[n, rows] = jnp.broadcast_to(top, (HD, HD))
        lanes_ref[n, rows] = lanes
        total_ref[n, rows] = mixed

    return emit


def attend_mine(meta_ref, q_ref, low, own_ref, high_ref, top_ref, lanes_ref, total_ref, s_even, s_odd):
    def fetch(which):
        def of(i, d, at):
            n = place(i, d)[0]
            return (low, own_ref, high_ref)[n // 4][(n % 4,) + at + (which,)]

        return of

    units = units_of(meta_ref, 0, fetch(0), fetch(1))
    attend(units, q_ref, (s_even, s_odd), biases(meta_ref), None, keep_in(top_ref, lanes_ref, total_ref))


def attend_theirs(
    meta_ref, q_ref, top_in, lanes_in, total_in, low, own_ref, high_ref, out_ref, k_ref, v_ref, s_even, s_odd, sems
):
    first = 1 - meta_ref[1]
    sources = ((low, first), (own_ref, first + 4), (high_ref, first + 8))

    def load(src, which, ref, slot, n):
        made = pltpu.make_async_copy(src.at[:, :, :, :, which], ref.at[pl.ds(slot, 4)], sems.at[n])
        made.start()
        return made

    k_copies = [load(src, 0, k_ref, slot, n) for n, (src, slot) in enumerate(sources)]
    v_copies = [load(src, 1, v_ref, slot, n + 3) for n, (src, slot) in enumerate(sources)]

    def fetch(ref):
        return lambda i, d, at: ref[(place(i, d)[0] + 1,) + at]

    def wait_values():
        for made in v_copies:
            made.wait()

    units = units_of(meta_ref, 1, fetch(k_ref), fetch(v_ref))

    def emit(n, rows, high, top, lanes, mixed):
        row_sum = jnp.sum(lanes, axis=1, keepdims=True)
        unit = units[n]
        out_ref[unit.i, :, high, unit.parity] = (mixed / row_sum).astype(jnp.bfloat16).reshape(2, TOK, HD)

    for made in k_copies:
        made.wait()
    state = (top_in, lanes_in, total_in)
    attend(units, q_ref, (s_even, s_odd), biases(meta_ref), state, emit, wait_values)


def side_by_side(x_ref, out_ref):
    for h in range(HEADS):
        out_ref[:, h * HD : (h + 1) * HD] = x_ref[h]


def call(kernel, out_shape, specs, flops=0, scratch=(), limit=VMEM_LIMIT, **more):
    params = pltpu.CompilerParams(vmem_limit_bytes=limit)
    cost = pl.CostEstimate(flops=flops, bytes_accessed=4 << 20, transcendentals=flops // 512)
    return pl.pallas_call(
        kernel, out_shape=out_shape, in_specs=specs, scratch_shapes=scratch,
        compiler_params=params, cost_estimate=cost, **more,
    )


def exchange(x):
    return lax.all_to_all(x, ("x", "y"), split_axis=0, concat_axis=0, tiled=True)


def local(queries, keys, values, q_gain, k_gain, block_offset):
    half = jnp.bfloat16
    tokens = pltpu.VMEM((TOK, HEADS * HD), half)
    kv = call(
        prepare_kv,
        jax.ShapeDtypeStruct((SLOTS, 2, TOK, HD), half),
        [ANYWHERE] * 3,
        scratch=[tokens, tokens, pltpu.VMEM((1, HEADS * HD), jnp.float32), pltpu.SemaphoreType.DMA((3,))],
        limit=PREPARE_LIMIT,
    )(keys, values, k_gain.reshape(1, -1))
    queries, block_offset, kv = lax.optimization_barrier((queries, block_offset, kv))
    z = lax.axis_index("z")
    core = lax.axis_index("c")
    frame = lax.dynamic_slice_in_dim(block_offset.reshape(8, 4, 2, 6), z, 1, 0)
    table = lax.dynamic_slice_in_dim(frame, core, 1, 2).reshape(24)
    meta = jnp.concatenate([jnp.stack([z, core]).astype(jnp.int32), table])
    q, meta = call(
        prepare_q,
        [jax.ShapeDtypeStruct((SLOTS, TOK, HD), half), jax.ShapeDtypeStruct((META,), jnp.int32)],
        [WHOLE] * 2 + [TABLE],
        out_specs=[WHOLE, TABLE],
    )(queries, q_gain.reshape(1, -1), meta)
    kv = exchange(kv)
    q, kv = lax.optimization_barrier((q, kv))
    blocks = (4, 2, 2, 2, TOK, HD)
    q = exchange(q).reshape(blocks)

    mine = kv.reshape(4, 2, 2, 2, 2, TOK, HD)
    swap = [(0, 1), (1, 0)]
    low = lax.ppermute(mine, "z", [(n, n + 1) for n in range(7)])
    high = lax.ppermute(mine, "z", [(n + 1, n) for n in range(7)])
    theirs = lax.ppermute(mine, "c", swap)
    their_low = lax.ppermute(low, "c", swap)
    their_high = lax.ppermute(high, "c", swap)
    scores = lambda columns: [pltpu.VMEM((256, columns), jnp.float32)] * 2
    state = call(
        attend_mine,
        [jax.ShapeDtypeStruct((8, 256, HD), jnp.float32)] * 3,
        [TABLE] + [WHOLE] * 4,
        flops=4 * 4 * 1536 * 512 * HD,
        scratch=scores(1536),
    )(meta, q, low, mine, high)
    kept = pltpu.VMEM((13, 2, 2, 2, TOK, HD), half)
    out = call(
        attend_theirs,
        jax.ShapeDtypeStruct(blocks, half),
        [TABLE] + [WHOLE] * 4 + [ANYWHERE] * 3,
        flops=4 * 4 * 2048 * 512 * HD,
        scratch=[kept, kept] + scores(2048) + [pltpu.SemaphoreType.DMA((6,))],
    )(meta, q, *state, their_low, theirs, their_high)
    back = exchange(out.reshape(SLOTS, TOK, HD))
    return call(side_by_side, jax.ShapeDtypeStruct((TOK, HEADS * HD), half), [WHOLE])(back)


def solution(mesh):
    grid = Mesh(mesh.devices.reshape(8, 4, 2, 8), ("z", "x", "c", "y"))
    tokens = P(("z", "x", "c", "y"), None)
    return jax.shard_map(
        local, mesh=grid, in_specs=(tokens,) * 3 + (P(),) * 3, out_specs=tokens, check_vma=False
    )
```

```python
import math

import jax
import jax.numpy as jnp
from jax import lax
from jax.experimental import pallas as pl
from jax.experimental.pallas import tpu as pltpu
from jax.sharding import Mesh
from jax.sharding import PartitionSpec as P

HD = 128
HEADS = 24
TOK = 64
SLOTS = 32
LOG2E = 1.4426950408889634
FACTOR = LOG2E / math.sqrt(HD)
VMEM_LIMIT = 48 * 1024 * 1024
PREPARE_LIMIT = 60 * 1024 * 1024
WHOLE = pl.BlockSpec(memory_space=pltpu.VMEM)
TABLE = pl.BlockSpec(memory_space=pltpu.SMEM)
ANYWHERE = pl.BlockSpec(memory_space=pl.ANY)


THEIRS = 13
OWN_FLOPS = 40 * 8704 * 512 * HD
FRAMES = 25
DISTANCES = (0, 1, -1, 2, -2, 3, -3, 4, -4, 6, -6, 5, -5, 7, -7)


def normed(x_ref, gain_ref):
    x = x_ref[...].astype(jnp.float32)
    mean_square = jnp.mean(x * x, axis=-1, keepdims=True)
    return (x * lax.rsqrt(mean_square + 1e-06) * gain_ref[...]).astype(jnp.bfloat16)


def spread(x, out_ref):
    for h in range(HEADS):
        out_ref[h] = x[:, h * HD : (h + 1) * HD]
    for h in range(HEADS, SLOTS):
        out_ref[h] = jnp.zeros(out_ref.shape[1:], out_ref.dtype)


def prepare_kv(k_hbm, v_hbm, gain_hbm, out_ref, k_ref, v_ref, gain_ref, sems):
    pairs = ((k_hbm, k_ref), (gain_hbm, gain_ref), (v_hbm, v_ref))
    loads = [pltpu.make_async_copy(src, dst, sems.at[n]) for n, (src, dst) in enumerate(pairs)]
    for load in loads:
        load.start()
    loads[0].wait()
    loads[1].wait()
    spread(normed(k_ref, gain_ref), out_ref.at[:, 0])
    loads[2].wait()
    spread(v_ref, out_ref.at[:, 1])


def prepare_q(q_ref, gain_ref, out_ref):
    spread(normed(q_ref, gain_ref), out_ref)


def lane_fold(op, matrix):
    parts = [matrix[:, n : n + HD] for n in range(0, matrix.shape[1], HD)]
    while len(parts) > 1:
        parts = [op(*parts[n : n + 2]) if n + 1 < len(parts) else parts[n] for n in range(0, len(parts), 2)]
    return parts[0]


def width(d):
    return 512 if abs(d) <= 1 else 256 if abs(d) <= 3 else 128


def place(i, d):
    if d % 2 == 0:
        n = 4 + i + d // 2
        return n, "low" if n < 4 else "high" if n >= 8 else None
    n = 4 + i + (d - 1) // 2
    return THEIRS + n, "low" if n < 3 else "edge_low" if n == 3 else "high" if n >= 8 else "edge_high" if n == 7 else None


class Unit:
    def __init__(self, meta_ref, i, parity, inside, keys, values):
        self.i = i
        self.parity = parity
        self.offs = [[meta_ref[2 + (i * 3 + level) * 2 + side] for side in range(2)] for level in range(3)]
        self.keys = keys
        self.values = values
        used = [d for d in DISTANCES if (place(i, d)[1] is None) == inside]
        self.both = []
        self.far = []
        for size, groups in ((512, self.both), (256, self.both), (128, self.far)):
            here = [d for d in used if width(d) == size]
            per = 512 // size
            groups += [here[n : n + per] for n in range(0, len(here), per)]

    def q(self, q_ref, high):
        return q_ref[self.i, :, high, self.parity].reshape(HD, HD)

    def gather(self, fetch, group, cls):
        parts = []
        for d in group:
            side = 0 if d < 0 else 1
            if abs(d) <= 1:
                at = (slice(None),) * 3
            elif abs(d) <= 3:
                at = (slice(None), slice(None), (cls + self.offs[1][side]) & 1)
            else:
                kept = (cls + self.offs[2][side]) & 3
                at = (slice(None), kept >> 1, kept & 1)
            parts.append(fetch(self.i, d, at).reshape(width(d), HD))
        return jnp.concatenate(parts, axis=0)


def store_scores(unit, q, group, cls, s_ref, rows, start, bias):
    key = unit.gather(unit.keys, group, cls)
    s = lax.dot_general(q, key, (((1,), (1,)), ((), ())), preferred_element_type=jnp.float32)
    if bias is not None:
        size = width(group[0])
        s = jnp.concatenate(
            [s[:, m * size : (m + 1) * size] + bias[place(unit.i, d)[1]] for m, d in enumerate(group)], axis=1
        )
    s_ref[rows, start : start + key.shape[0]] = s
    return lane_fold(jnp.maximum, s), start + key.shape[0]


def score(unit, q_ref, s_ref, before=None, bias=None):
    q = [unit.q(q_ref, high) for high in range(2)]
    both = jnp.concatenate(q, axis=0)
    top = before
    start = 0
    for group in unit.both:
        part, start = store_scores(unit, both, group, unit.parity, s_ref, slice(0, 256), start, bias)
        top = part if top is None else jnp.maximum(top, part)
    tops = []
    for high in range(2):
        rows = slice(high * HD, (high + 1) * HD)
        own = top[rows]
        at = start
        for group in unit.far:
            part, at = store_scores(unit, q[high], group, unit.parity + 2 * high, s_ref, rows, at, bias)
            own = jnp.maximum(own, part)
        tops.append(jnp.max(own, axis=1, keepdims=True))
    return tops


def mix(unit, tops, s_ref):
    shift = jnp.concatenate(tops, axis=0) * FACTOR
    sums = {}

    def weigh(rows, start, group, moved):
        size = width(group[0])
        weights = jnp.exp2(s_ref[rows, start : start + size * len(group)] * FACTOR - moved)
        key = (rows.start, rows.stop)
        for m in range(len(group)):
            part = lane_fold(jnp.add, weights[:, m * size : (m + 1) * size])
            sums[key] = sums[key] + part if key in sums else part
        return weights.astype(jnp.bfloat16)

    total = None
    start = 0
    for group in unit.both:
        w = weigh(slice(0, 256), start, group, shift)
        start += w.shape[1]
        mixed = jnp.dot(w, unit.gather(unit.values, group, unit.parity), preferred_element_type=jnp.float32)
        total = mixed if total is None else total + mixed
    result = []
    for high in range(2):
        rows = slice(high * HD, (high + 1) * HD)
        own = total[rows]
        at = start
        for group in unit.far:
            w = weigh(rows, at, group, shift[rows])
            at += w.shape[1]
            value = unit.gather(unit.values, group, unit.parity + 2 * high)
            own = own + jnp.dot(w, value, preferred_element_type=jnp.float32)
        lanes = None
        for (first, last), part in sums.items():
            if not first <= rows.start < last:
                continue
            if last - first == 256:
                part = part[rows]
            lanes = part if lanes is None else lanes + part
        result.append((lanes, own))
    return result


def attend_own(meta_ref, q_ref, mine_ref, theirs_ref, top_ref, lanes_ref, total_ref, s_even, s_odd):
    core = meta_ref[1]

    def fetch(which):
        def of(i, d, at):
            n = place(i, d)[0]
            ref, n = (mine_ref, n - 4) if d % 2 == 0 else (theirs_ref, n - THEIRS - 4 + core)
            return ref[(n,) + at + (which,)]

        return of

    units = [Unit(meta_ref, i, parity, True, fetch(0), fetch(1)) for i in range(4) for parity in range(2)]
    s_refs = (s_even, s_odd)
    tops = score(units[0], q_ref, s_refs[0])
    for n, unit in enumerate(units):
        now = tops
        if n + 1 < len(units):
            tops = score(units[n + 1], q_ref, s_refs[(n + 1) % 2])
        for high, (lanes, own) in enumerate(mix(unit, now, s_refs[n % 2])):
            rows = slice(high * HD, (high + 1) * HD)
            top_ref[n, rows] = jnp.broadcast_to(now[high], (HD, HD))
            lanes_ref[n, rows] = lanes
            total_ref[n, rows] = own


def attend_rest(
    meta_ref, q_ref, top_ref, lanes_ref, total_ref, low, high_ref, their_own, their_low, their_high,
    out_ref, k_ref, v_ref, s_even, s_odd, sems,
):
    z = meta_ref[0]
    core = meta_ref[1]
    sources = ((low, 0), (high_ref, 8), (their_low, THEIRS - core), (their_own, THEIRS - core + 4),
               (their_high, THEIRS - core + 8))

    def load(src, which, ref, slot, n):
        made = pltpu.make_async_copy(src.at[:, :, :, :, which], ref.at[pl.ds(slot, 4)], sems.at[n])
        made.start()
        return made

    k_copies = [load(src, 0, k_ref, slot, n) for n, (src, slot) in enumerate(sources)]
    v_copies = [load(src, 1, v_ref, slot, n + 5) for n, (src, slot) in enumerate(sources)]
    bias = {}
    for kind, usable in (
        ("low", z > 0),
        ("edge_low", (z > 0) | (core == 1)),
        ("edge_high", (z < 7) | (core == 0)),
        ("high", z < 7),
    ):
        bias[kind] = jnp.where(usable, 0.0, -1e30).astype(jnp.float32)

    def keys(i, d, at):
        return k_ref[(place(i, d)[0],) + at]

    def values(i, d, at):
        return v_ref[(place(i, d)[0],) + at]

    units = [Unit(meta_ref, i, parity, False, keys, values) for i in range(4) for parity in range(2)]
    s_refs = (s_even, s_odd)
    for made in k_copies:
        made.wait()
    tops = score(units[0], q_ref, s_refs[0], top_ref[0], bias)
    for made in v_copies:
        made.wait()
    for n, unit in enumerate(units):
        now = tops
        if n + 1 < len(units):
            tops = score(units[n + 1], q_ref, s_refs[(n + 1) % 2], top_ref[n + 1], bias)
        for high, (lanes, mixed) in enumerate(mix(unit, now, s_refs[n % 2])):
            rows = slice(high * HD, (high + 1) * HD)
            carried = jnp.exp2((top_ref[n, rows] - now[high]) * FACTOR)
            lanes = lanes + lanes_ref[n, rows] * carried
            mixed = mixed + total_ref[n, rows] * carried
            row_sum = jnp.sum(lanes, axis=1, keepdims=True)
            out_ref[unit.i, :, high, unit.parity] = (mixed / row_sum).astype(jnp.bfloat16).reshape(2, TOK, HD)


def side_by_side(x_ref, out_ref):
    for h in range(HEADS):
        out_ref[:, h * HD : (h + 1) * HD] = x_ref[h]


def call(kernel, out_shape, specs, flops=0, scratch=(), limit=VMEM_LIMIT, **more):
    params = pltpu.CompilerParams(vmem_limit_bytes=limit)
    cost = pl.CostEstimate(flops=flops, bytes_accessed=4 << 20, transcendentals=flops // 512)
    return pl.pallas_call(
        kernel, out_shape=out_shape, in_specs=specs, scratch_shapes=scratch,
        compiler_params=params, cost_estimate=cost, **more,
    )


def exchange(x):
    return lax.all_to_all(x, ("x", "y"), split_axis=0, concat_axis=0, tiled=True)


def local(queries, keys, values, q_gain, k_gain, block_offset):
    half = jnp.bfloat16
    z = lax.axis_index("z")
    core = lax.axis_index("c")
    frame = lax.dynamic_slice_in_dim(block_offset.reshape(8, 4, 2, 6), z, 1, 0)
    table = lax.dynamic_slice_in_dim(frame, core, 1, 2).reshape(24)
    meta = jnp.concatenate([jnp.stack([z, core]).astype(jnp.int32), table])

    tokens = pltpu.VMEM((TOK, HEADS * HD), half)
    kv = call(
        prepare_kv,
        jax.ShapeDtypeStruct((SLOTS, 2, TOK, HD), half),
        [ANYWHERE] * 3,
        scratch=[tokens, tokens, pltpu.VMEM((1, HEADS * HD), jnp.float32), pltpu.SemaphoreType.DMA((3,))],
        limit=PREPARE_LIMIT,
    )(keys, values, k_gain.reshape(1, -1))
    queries, kv = lax.optimization_barrier((queries, kv))
    q = call(prepare_q, jax.ShapeDtypeStruct((SLOTS, TOK, HD), half), [WHOLE] * 2)(queries, q_gain.reshape(1, -1))
    kv = exchange(kv)
    q, kv = lax.optimization_barrier((q, kv))
    blocks = (4, 2, 2, 2, TOK, HD)
    q = exchange(q).reshape(blocks)

    mine = kv.reshape(4, 2, 2, 2, 2, TOK, HD)
    swap = [(0, 1), (1, 0)]
    low = lax.ppermute(mine, "z", [(n, n + 1) for n in range(7)])
    high = lax.ppermute(mine, "z", [(n + 1, n) for n in range(7)])
    theirs = lax.ppermute(mine, "c", swap)
    their_low = lax.ppermute(low, "c", swap)
    their_high = lax.ppermute(high, "c", swap)

    scores = [pltpu.VMEM((256, 2560), jnp.float32)] * 2
    state = [jax.ShapeDtypeStruct((8, 256, HD), jnp.float32)] * 3
    state = call(attend_own, state, [TABLE] + [WHOLE] * 3, flops=OWN_FLOPS, scratch=scores)(meta, q, mine, theirs)
    kept = pltpu.VMEM((FRAMES, 2, 2, 2, TOK, HD), half)
    out = call(
        attend_rest,
        jax.ShapeDtypeStruct(blocks, half),
        [TABLE] + [WHOLE] * 4 + [ANYWHERE] * 5,
        flops=4 * 5632 * 512 * HD,
        scratch=[kept, kept] + scores + [pltpu.SemaphoreType.DMA((10,))],
    )(meta, q, *state, low, high, theirs, their_low, their_high)
    back = exchange(out.reshape(SLOTS, TOK, HD))
    return call(side_by_side, jax.ShapeDtypeStruct((TOK, HEADS * HD), half), [WHOLE])(back)


def solution(mesh):
    grid = Mesh(mesh.devices.reshape(8, 4, 2, 8), ("z", "x", "c", "y"))
    tokens = P(("z", "x", "c", "y"), None)
    return jax.shard_map(
        local, mesh=grid, in_specs=(tokens,) * 3 + (P(),) * 3, out_specs=tokens, check_vma=False
    )
```
